32 devices in a mesh: mod: 16 (over z, y, x), pair: 2 (over core).
Axes of the slice: x: 2, y: 2, z: 4, core: 2. Of those that a mesh axis runs over, the one named last changes fastest.
Arguments:
- query_grads: bfloat16 [128, 64, 16, 128], P(('mod', 'pair')), may hold values from -6 to 6
- train_grads: bfloat16 [1024, 64, 16, 128], P('pair', 'mod'), may hold values from -6 to 6
- left_basis: bfloat16 [64, 16, 16], P('mod'), may hold values from -1.5 to 1.5
- right_basis: bfloat16 [64, 128, 128], P('mod'), may hold values from -0.5 to 0.5
- eigenvalues: bfloat16 [64, 16, 128], P('mod'), may hold values from 0.0009994507 to 10
- block_rows: int32 [64], P('mod'), may hold values from 0 to 16, as said below
Outputs:
- scores: float32 [128, 1024], P('mod', 'pair')
The draws below stay inside these ranges and needn't reach their ends.
Inputs may be any that keep to these rules, and one draw needn't show every extreme that they name: `block_rows`: owner j of the 16 owners holds slots j * 4 to (j + 1) * 4 - 1; of these the first 1 to 4 are live with 8 to 16 rows each and the rest hold 0; some owner has all 4 slots live and a slot of 16 rows, and some live slot has 8 rows.
All inputs are finite; a program needn't handle non-finite values.
Results may differ from the reference program's by a relative error of at most 0.0047.
Values may be sent and summed in bfloat16 or wider, within the bound.
A program may use at most 128 MiB of HBM per device.

```python
import math
import jax
import jax.numpy as jnp
from jax import lax

COLS = 128
ROWS = 16
SLOTS = 4
TOTAL_SLOTS = 64
QUERIES = 128
TRAIN = 1024


def draw_block_rows(key, part):
    owners = TOTAL_SLOTS // SLOTS
    keys = jax.random.split(jax.random.fold_in(key, 7), 4)
    counts = jax.random.randint(keys[0], (owners,), 1, SLOTS + 1)
    busiest = jax.random.randint(keys[1], (), 0, owners)
    counts = counts.at[busiest].set(SLOTS)
    widths = jax.random.randint(keys[2], (owners, SLOTS), 8, ROWS + 1)
    narrow = (busiest + 1 + jax.random.randint(keys[3], (), 0, owners - 1)) % owners
    widths = widths.at[busiest, 0].set(ROWS).at[narrow, 0].set(8)
    live = jnp.arange(SLOTS)[None, :] < counts[:, None]
    return jnp.where(live, widths, 0).astype(jnp.int32).reshape(TOTAL_SLOTS)


def strengthened(drawn, key, source, target, parts, factor):
    owner, partner = [(jnp.arange(drawn.shape[axis_at]) // (drawn.shape[axis_at] // parts)).reshape([-1 if axis == axis_at else 1 for axis in range(drawn.ndim)]) for axis_at in (source, target)]
    chosen = jax.random.permutation(key, parts)[partner]
    strong = (owner == chosen) | (owner == (partner + parts // 2) % parts)
    return jnp.where(strong, factor * drawn, drawn)


def block_scale(stream_key, shape, pieces, least, largest):
    def one(axis_at, blocks):
        steps = jax.random.uniform(jax.random.fold_in(jax.random.fold_in(stream_key, 6), axis_at), (blocks,), jnp.float32, least / len(pieces), largest / len(pieces))
        return jnp.repeat(jnp.exp(steps), shape[axis_at] // blocks).reshape((-1,) + (1,) * (len(shape) - axis_at - 1))

    level = one(*pieces[0])
    for cut in pieces[1:]:
        level = level * one(*cut)
    return level


def noise(key, dims, scale, most, shards=(), held_as=jnp.bfloat16):
    values = jax.random.normal(key, dims, jnp.float32) * scale
    if len(shards) > 0:
        values = block_scale(key, dims, shards, -0.22, 0.18) * values
    return jnp.clip(values, min=-most, max=most).astype(held_as)


def bell_draw_with(own_key, shape, spread, limit, pieces, heavy, kind=jnp.bfloat16):
    entries = spread * jax.random.normal(own_key, shape, jnp.float32)
    if pieces:
        entries = entries * block_scale(own_key, shape, pieces, -0.22, 0.18)
    return jnp.clip(strengthened(entries, jax.random.fold_in(own_key, 3), *heavy), -limit, limit).astype(kind)


def setup_inputs(seed: int = 0) -> dict:
    key_of = jax.random.split(jax.random.key(seed), 7)
    query_grads = bell_draw_with(key_of[0], (QUERIES, TOTAL_SLOTS, ROWS, COLS), 1.0, 6.0, ((0, 32),), (1, 0, 32, 2.75))
    train_grads = noise(key_of[1], (TRAIN, TOTAL_SLOTS, ROWS, COLS), 1.0, 6.0, ((0, 2), (1, 16)))
    left_basis = noise(key_of[2], (TOTAL_SLOTS, ROWS, ROWS), ROWS ** -0.5, 1.5, ((0, 16),))
    right_basis = noise(key_of[3], (TOTAL_SLOTS, COLS, COLS), COLS ** -0.5, 0.5, ((0, 16),))
    eigenvalues = jnp.clip(jnp.exp(math.log(10.0) - 9.21089 * jax.random.uniform(key_of[4], (TOTAL_SLOTS, ROWS, COLS), jnp.float32) ** block_scale(key_of[4], (TOTAL_SLOTS, ROWS, COLS), ((0, 16),), -0.2, 0.2)), 0.0009994507, 10.0).astype(jnp.bfloat16)
    block_rows = draw_block_rows(jax.random.fold_in(key_of[6], 71), 0)
    return dict(query_grads=query_grads, train_grads=train_grads, left_basis=left_basis, right_basis=right_basis, eigenvalues=eigenvalues, block_rows=block_rows)


def precondition(grad_slot, left_factor, right_factor, eig_block, live_rows):
    count_n, row_total, col_total = grad_slot.shape
    row_mask = (jnp.arange(row_total) < live_rows).astype(jnp.float32)
    left_masked = (left_factor.astype(jnp.float32) * row_mask[:, None] * row_mask[None, :]).astype(jnp.bfloat16)
    masked_grads = (grad_slot.astype(jnp.float32) * row_mask[None, :, None]).astype(jnp.bfloat16)
    rotated_right = jnp.dot(masked_grads.reshape(count_n * row_total, col_total), right_factor, preferred_element_type=jnp.float32).astype(jnp.bfloat16).reshape(count_n, row_total, col_total)
    rotated = jnp.einsum('ba,nbc->nac', left_masked.astype(jnp.float32), rotated_right.astype(jnp.float32))
    eig_float = eig_block.astype(jnp.float32)
    damping = 0.1 * jnp.sum(eig_float * row_mask[:, None]) / jnp.maximum(live_rows * col_total, 1).astype(jnp.float32)
    scaled = (rotated / (eig_float + damping)).astype(jnp.bfloat16)
    back_right = jnp.dot(scaled.reshape(count_n * row_total, col_total), right_factor.T, preferred_element_type=jnp.float32).astype(jnp.bfloat16).reshape(count_n, row_total, col_total)
    return jnp.einsum('ab,nbc->nac', left_masked.astype(jnp.float32), back_right.astype(jnp.float32)).astype(jnp.bfloat16)

def reference(query_grads, train_grads, left_basis, right_basis, eigenvalues, block_rows):
    query_count = query_grads.shape[0]
    train_count = train_grads.shape[0]
    slot_total = query_grads.shape[1]
    norm_scale = 1.0 / math.sqrt(slot_total * query_grads.shape[2] * query_grads.shape[3])

    def slot_step(slot_index, totals):
        grad_slot = lax.dynamic_index_in_dim(query_grads, slot_index, 1, keepdims=False)
        train_slot = lax.dynamic_index_in_dim(train_grads, slot_index, 1, keepdims=False)
        result = precondition(grad_slot, left_basis[slot_index], right_basis[slot_index], eigenvalues[slot_index], block_rows[slot_index])
        return totals + lax.dot_general(result.reshape(query_count, -1), train_slot.reshape(train_count, -1), (((1,), (1,)), ((), ())), preferred_element_type=jnp.float32)
    totals = lax.fori_loop(0, slot_total, slot_step, jnp.zeros((query_count, train_count), jnp.float32))
    return totals * norm_scale
```

```python
import functools
import math

import jax
import jax.numpy as jnp
from jax import lax
from jax.experimental import pallas as pl
from jax.experimental.pallas import tpu as pltpu
from jax.sharding import PartitionSpec as P

MESH = pl.DeviceIdType.MESH
GROUP = 16
F32 = jnp.float32
BF16 = jnp.bfloat16


def iota(shape, dim):
    return lax.broadcasted_iota(jnp.int32, shape, dim)


def dot(a, b):
    return jnp.dot(a, b, preferred_element_type=F32)


def dot_t(a, b):
    return lax.dot_general(a, b, (((1,), (1,)), ((), ())), preferred_element_type=F32)


def turn(rows, right, mixer):
    half = rows.shape[0] // 2
    rotated_right = dot(rows, right).astype(BF16)
    side = jnp.concatenate([rotated_right[:half], rotated_right[half:]], axis=1)
    return dot(mixer, side)


def kernel(
    n,
    q_ref, t_ref, left_ref, right_ref, eig_ref, rows_ref,
    out_ref,
    recv, tv, tr, sc, mixer, recip, acc, perm, msg, got,
    send_sem, recv_sem, t_sem, pair_send, pair_recv, msg_send, msg_recv,
):
    per, _, rows, cols = q_ref.shape
    trains, slots = t_ref.shape[0], t_ref.shape[1]
    queries = n * per
    me = lax.axis_index("mod")
    side = lax.axis_index("pair")
    other = 1 - side

    def peer(i):
        return lax.rem(me + 1 + lax.rem(n // 2 - 1 + i, n - 1), n)

    barrier = pltpu.get_barrier_semaphore()

    def greet(i, carry):
        pl.semaphore_signal(barrier, inc=1, device_id=(peer(i), side), device_id_type=MESH)
        return carry

    lax.fori_loop(0, n - 1, greet, 0)
    pl.semaphore_signal(barrier, inc=1, device_id=(me, other), device_id_type=MESH)

    parts = t_sem.shape[0]
    part = trains // parts

    def train_copy(i):
        return pltpu.make_async_copy(
            t_ref.at[pl.ds(i * part, part)], tv.at[pl.ds(i * part, part)], t_sem.at[i]
        )

    for i in range(parts):
        train_copy(i).start()

    pl.semaphore_wait(barrier, n)

    for k in range(slots):
        def send(i, carry, k=k):
            to = peer(i)
            pltpu.make_async_remote_copy(
                src_ref=q_ref.at[:, to * slots + k],
                dst_ref=recv.at[k, pl.ds(me * per, per)],
                send_sem=send_sem,
                recv_sem=recv_sem.at[k],
                device_id=(to, side),
                device_id_type=MESH,
            ).start()
            return carry

        lax.fori_loop(0, n - 1, send, 0)
        pltpu.make_async_copy(
            q_ref.at[:, me * slots + k], recv.at[k, pl.ds(me * per, per)], recv_sem.at[k]
        ).start()

    big = GROUP * rows
    pick_a = (iota((big, rows), 0) // GROUP == iota((big, rows), 1)).astype(BF16)
    pick_b = (lax.rem(iota((rows, big), 1), rows) == iota((rows, big), 0)).astype(BF16)
    same = lax.rem(iota((big, big), 0), GROUP) == iota((big, big), 1) // rows
    for s in range(slots):
        live = rows_ref[s]
        keep = (iota((rows, rows), 0) < live) & (iota((rows, rows), 1) < live)
        left = jnp.where(keep, left_ref[s].astype(F32), 0.0).astype(BF16)
        spread = dot(dot_t(pick_a, left).astype(BF16), pick_b)
        mixer[s] = jnp.where(same, spread, 0.0).astype(BF16)
        eig = eig_ref[s].astype(F32)
        kept = jnp.where(iota((rows, cols), 0) < live, eig, 0.0)
        width = jnp.maximum(live * cols, 1).astype(F32)
        damping = 0.1 * jnp.sum(jnp.sum(kept, axis=1, keepdims=True), axis=0, keepdims=True) / width
        inverse = 1.0 / (eig + damping)
        for a in range(rows):
            block = jnp.broadcast_to(inverse[a : a + 1], (GROUP, cols))
            recip[s, a * GROUP : (a + 1) * GROUP] = jnp.concatenate([block, block], axis=1)

    wide = trains // 2
    total = perm.shape[0]
    out_row = iota((total, total), 0)
    in_row = iota((total, total), 1)
    owner = out_row // (4 * per)
    column_half = lax.rem(out_row // (2 * per), 2)
    far = lax.rem(lax.rem(out_row // per, 2) + side, 2)
    want = ((column_half * 2 + far) * n + owner) * per + lax.rem(out_row, per)
    perm[...] = (in_row == want).astype(BF16)

    def rotate_train(step, carry):
        base = step * 2 * GROUP
        for s in range(slots):
            block = tv[pl.ds(base, 2 * GROUP), s].reshape(2 * big, cols)
            turned = turn(block, right_ref[s], mixer[s]).astype(BF16)
            for half in range(2):
                for a in range(rows):
                    tr[s, pl.ds(pl.multiple_of(base + half * GROUP, GROUP), GROUP), a * cols : (a + 1) * cols] = turned[
                        a * GROUP : (a + 1) * GROUP, half * cols : (half + 1) * cols
                    ]
        return carry

    for i in range(parts):
        train_copy(i).wait()
        steps = part // (2 * GROUP)
        lax.fori_loop(i * steps, (i + 1) * steps, rotate_train, 0)

    def exchange(k):
        return pltpu.make_async_remote_copy(
            src_ref=sc.at[k, 0],
            dst_ref=sc.at[k, 1],
            send_sem=pair_send.at[k],
            recv_sem=pair_recv.at[k],
            device_id=(me, other),
            device_id_type=MESH,
        )

    acc[...] = jnp.zeros_like(acc)
    for k in range(slots):
        pltpu.make_async_copy(recv.at[k], recv.at[k], recv_sem.at[k]).wait()
        mask = (iota((rows, cols), 0) < rows_ref[k]).astype(F32).astype(BF16)
        for g in range(queries // (2 * GROUP)):
            base = g * 2 * GROUP
            block = (recv[k, base : base + 2 * GROUP] * mask[None]).reshape(2 * big, cols)
            scaled = (turn(block, right_ref[k], mixer[k]) * recip[k]).astype(BF16)
            for half in range(2):
                for a in range(rows):
                    sc[k, 0, base + half * GROUP : base + (half + 1) * GROUP, a * cols : (a + 1) * cols] = scaled[
                        a * GROUP : (a + 1) * GROUP, half * cols : (half + 1) * cols
                    ]
        exchange(k).start()
        if k > 0:
            exchange(k - 1).wait()
            both = sc[k - 1].reshape(2 * queries, rows * cols)
            acc[...] += dot_t(both, tr[k - 1])
    last = slots - 1
    acc[:queries] += dot_t(sc[last, 0], tr[last])
    exchange(last).wait()
    acc[queries:] += dot_t(sc[last, 1], tr[last])

    stacked = jnp.concatenate([acc[:, :wide], acc[:, wide:]], axis=0).astype(BF16)
    msg[...] = dot(perm[...], stacked).astype(BF16).reshape(msg.shape)

    def post(i, carry):
        to = peer(i)
        pltpu.make_async_remote_copy(
            src_ref=msg.at[to],
            dst_ref=got.at[me],
            send_sem=msg_send,
            recv_sem=msg_recv,
            device_id=(to, side),
            device_id_type=MESH,
        ).start()
        return carry

    lax.fori_loop(0, n - 1, post, 0)
    pltpu.make_async_copy(msg.at[me], got.at[me], msg_recv).start()
    sent = q_ref.at[:, pl.ds(0, (n - 1) * slots)]
    pltpu.make_async_copy(sent, sent, send_sem).wait()
    pltpu.make_async_copy(got, got, msg_recv).wait()
    summed = jnp.sum(got[...].astype(F32), axis=0)
    out_ref[:, :wide] = summed[: 2 * per]
    out_ref[:, wide:] = summed[2 * per :]
    posted = msg.at[pl.ds(0, n - 1)]
    pltpu.make_async_copy(posted, posted, msg_send).wait()


def on_device(n, query_grads, train_grads, left_basis, right_basis, eigenvalues, block_rows):
    per, slot_total, rows, cols = query_grads.shape
    trains, slots = train_grads.shape[:2]
    queries = n * per
    big = GROUP * rows
    wide = trains // 2
    norm_scale = 1.0 / math.sqrt(slot_total * rows * cols)
    vmem = pl.BlockSpec(memory_space=pltpu.VMEM)
    parts = pl.BlockSpec(memory_space=pl.ANY)
    dma = pltpu.SemaphoreType.DMA
    scores = pl.pallas_call(
        functools.partial(kernel, n),
        out_shape=jax.ShapeDtypeStruct((2 * per, trains), F32),
        in_specs=[parts, parts, vmem, vmem, vmem, pl.BlockSpec(memory_space=pltpu.SMEM)],
        out_specs=vmem,
        scratch_shapes=[
            pltpu.VMEM((slots, queries, rows, cols), BF16),
            pltpu.VMEM((trains, slots, rows, cols), BF16),
            pltpu.VMEM((slots, trains, rows * cols), BF16),
            pltpu.VMEM((slots, 2, queries, rows * cols), BF16),
            pltpu.VMEM((slots, big, big), BF16),
            pltpu.VMEM((slots, big, 2 * cols), F32),
            pltpu.VMEM((2 * queries, trains), F32),
            pltpu.VMEM((4 * queries, 4 * queries), BF16),
            pltpu.VMEM((n, 4 * per, wide), BF16),
            pltpu.VMEM((n, 4 * per, wide), BF16),
            dma,
            dma((slots,)),
            dma((4,)),
            dma((slots,)),
            dma((slots,)),
            dma,
            dma,
        ],
        compiler_params=pltpu.CompilerParams(
            collective_id=0, has_side_effects=True, vmem_limit_bytes=50 * 1024 * 1024
        ),
    )(query_grads, train_grads, left_basis, right_basis, eigenvalues, block_rows)
    return scores * norm_scale


def solution(mesh):
    placed = (
        P(("mod", "pair"), None, None, None),
        P("pair", "mod", None, None),
        P("mod", None, None),
        P("mod", None, None),
        P("mod", None, None),
        P("mod"),
    )
    return jax.shard_map(
        functools.partial(on_device, mesh.shape["mod"]),
        mesh=mesh,
        in_specs=placed,
        out_specs=P("mod", "pair"),
        check_vma=False,
    )
```

```python
import functools
import math

import jax
import jax.numpy as jnp
from jax import lax
from jax.experimental import pallas as pl
from jax.experimental.pallas import tpu as pltpu
from jax.sharding import PartitionSpec as P

MESH = pl.DeviceIdType.MESH
GROUP = 16
F32 = jnp.float32
BF16 = jnp.bfloat16


def iota(shape, dim):
    return lax.broadcasted_iota(jnp.int32, shape, dim)


def dot(a, b):
    return jnp.dot(a, b, preferred_element_type=F32)


def dot_t(a, b):
    return lax.dot_general(a, b, (((1,), (1,)), ((), ())), preferred_element_type=F32)


def turn(rows, right, mixer):
    half = rows.shape[0] // 2
    rotated_right = dot(rows, right).astype(BF16)
    side = jnp.concatenate([rotated_right[:half], rotated_right[half:]], axis=1)
    return dot(mixer, side)


def kernel(
    n,
    q_ref, t_ref, left_in, right_in, eig_in, rows_in,
    out_ref,
    left_ref, right_ref, eig_ref, rows_ref, recv, tv, tr, sc, mixer, recip, acc, perm, msg, got,
    small_sem, send_sem, recv_sem, t_sem, pair_send, pair_recv, msg_send, msg_recv,
):
    per, _, rows, cols = q_ref.shape
    trains, slots = t_ref.shape[0], t_ref.shape[1]
    queries = n * per
    me = lax.axis_index("mod")
    side = lax.axis_index("pair")
    other = 1 - side

    def peer(i):
        return lax.rem(me + 1 + lax.rem(n // 2 - 1 + i, n - 1), n)

    barrier = pltpu.get_barrier_semaphore()

    def greet(i, carry):
        pl.semaphore_signal(barrier, inc=1, device_id=(peer(i), side), device_id_type=MESH)
        return carry

    lax.fori_loop(0, n - 1, greet, 0)
    pl.semaphore_signal(barrier, inc=1, device_id=(me, other), device_id_type=MESH)

    parts = t_sem.shape[0]
    part = trains // parts

    def train_copy(i):
        return pltpu.make_async_copy(
            t_ref.at[pl.ds(i * part, part)], tv.at[pl.ds(i * part, part)], t_sem.at[i]
        )

    smalls = [
        pltpu.make_async_copy(source, target, small_sem.at[i])
        for i, (source, target) in enumerate(
            [(left_in, left_ref), (eig_in, eig_ref), (rows_in, rows_ref), (right_in, right_ref)]
        )
    ]
    for copy in smalls:
        copy.start()
    for i in range(parts):
        train_copy(i).start()

    pl.semaphore_wait(barrier, n)

    for k in range(slots):
        def send(i, carry, k=k):
            to = peer(i)
            pltpu.make_async_remote_copy(
                src_ref=q_ref.at[:, to * slots + k],
                dst_ref=recv.at[k, pl.ds(me * per, per)],
                send_sem=send_sem,
                recv_sem=recv_sem.at[k],
                device_id=(to, side),
                device_id_type=MESH,
            ).start()
            return carry

        lax.fori_loop(0, n - 1, send, 0)
        pltpu.make_async_copy(
            q_ref.at[:, me * slots + k], recv.at[k, pl.ds(me * per, per)], recv_sem.at[k]
        ).start()

    for copy in smalls:
        copy.wait()
    big = GROUP * rows
    pick_a = (iota((big, rows), 0) // GROUP == iota((big, rows), 1)).astype(BF16)
    pick_b = (lax.rem(iota((rows, big), 1), rows) == iota((rows, big), 0)).astype(BF16)
    same = lax.rem(iota((big, big), 0), GROUP) == iota((big, big), 1) // rows
    for s in range(slots):
        live = rows_ref[s]
        keep = (iota((rows, rows), 0) < live) & (iota((rows, rows), 1) < live)
        left = jnp.where(keep, left_ref[s].astype(F32), 0.0).astype(BF16)
        spread = dot(dot_t(pick_a, left).astype(BF16), pick_b)
        mixer[s] = jnp.where(same, spread, 0.0).astype(BF16)
        eig = eig_ref[s].astype(F32)
        kept = jnp.where(iota((rows, cols), 0) < live, eig, 0.0)
        width = jnp.maximum(live * cols, 1).astype(F32)
        damping = 0.1 * jnp.sum(jnp.sum(kept, axis=1, keepdims=True), axis=0, keepdims=True) / width
        inverse = 1.0 / (eig + damping)
        for a in range(rows):
            block = jnp.broadcast_to(inverse[a : a + 1], (GROUP, cols))
            recip[s, a * GROUP : (a + 1) * GROUP] = jnp.concatenate([block, block], axis=1)

    wide = trains // 2
    total = perm.shape[0]
    out_row = iota((total, total), 0)
    in_row = iota((total, total), 1)
    owner = out_row // (4 * per)
    column_half = lax.rem(out_row // (2 * per), 2)
    far = lax.rem(lax.rem(out_row // per, 2) + side, 2)
    want = ((column_half * 2 + far) * n + owner) * per + lax.rem(out_row, per)
    perm[...] = (in_row == want).astype(BF16)

    def rotate_train(step, carry):
        base = step * 2 * GROUP
        for s in range(slots):
            block = tv[pl.ds(base, 2 * GROUP), s].reshape(2 * big, cols)
            turned = turn(block, right_ref[s], mixer[s]).astype(BF16)
            for half in range(2):
                for a in range(rows):
                    tr[s, pl.ds(pl.multiple_of(base + half * GROUP, GROUP), GROUP), a * cols : (a + 1) * cols] = turned[
                        a * GROUP : (a + 1) * GROUP, half * cols : (half + 1) * cols
                    ]
        return carry

    for i in range(parts):
        train_copy(i).wait()
        steps = part // (2 * GROUP)
        lax.fori_loop(i * steps, (i + 1) * steps, rotate_train, 0)

    def exchange(k):
        return pltpu.make_async_remote_copy(
            src_ref=sc.at[k, 0],
            dst_ref=sc.at[k, 1],
            send_sem=pair_send.at[k],
            recv_sem=pair_recv.at[k],
            device_id=(me, other),
            device_id_type=MESH,
        )

    acc[...] = jnp.zeros_like(acc)
    for k in range(slots):
        pltpu.make_async_copy(recv.at[k], recv.at[k], recv_sem.at[k]).wait()
        mask = (iota((rows, cols), 0) < rows_ref[k]).astype(F32).astype(BF16)
        for g in range(queries // (2 * GROUP)):
            base = g * 2 * GROUP
            block = (recv[k, base : base + 2 * GROUP] * mask[None]).reshape(2 * big, cols)
            scaled = (turn(block, right_ref[k], mixer[k]) * recip[k]).astype(BF16)
            for half in range(2):
                for a in range(rows):
                    sc[k, 0, base + half * GROUP : base + (half + 1) * GROUP, a * cols : (a + 1) * cols] = scaled[
                        a * GROUP : (a + 1) * GROUP, half * cols : (half + 1) * cols
                    ]
        exchange(k).start()
        if k > 0:
            exchange(k - 1).wait()
            both = sc[k - 1].reshape(2 * queries, rows * cols)
            acc[...] += dot_t(both, tr[k - 1])
    last = slots - 1
    acc[:queries] += dot_t(sc[last, 0], tr[last])
    exchange(last).wait()
    acc[queries:] += dot_t(sc[last, 1], tr[last])

    stacked = jnp.concatenate([acc[:, :wide], acc[:, wide:]], axis=0).astype(BF16)
    msg[...] = dot(perm[...], stacked).astype(BF16).reshape(msg.shape)

    def post(i, carry):
        to = peer(i)
        pltpu.make_async_remote_copy(
            src_ref=msg.at[to],
            dst_ref=got.at[me],
            send_sem=msg_send,
            recv_sem=msg_recv,
            device_id=(to, side),
            device_id_type=MESH,
        ).start()
        return carry

    lax.fori_loop(0, n - 1, post, 0)
    pltpu.make_async_copy(msg.at[me], got.at[me], msg_recv).start()
    sent = q_ref.at[:, pl.ds(0, (n - 1) * slots)]
    pltpu.make_async_copy(sent, sent, send_sem).wait()
    pltpu.make_async_copy(got, got, msg_recv).wait()
    summed = jnp.sum(got[...].astype(F32), axis=0)
    out_ref[:, :wide] = summed[: 2 * per]
    out_ref[:, wide:] = summed[2 * per :]
    posted = msg.at[pl.ds(0, n - 1)]
    pltpu.make_async_copy(posted, posted, msg_send).wait()


def on_device(n, query_grads, train_grads, left_basis, right_basis, eigenvalues, block_rows):
    per, slot_total, rows, cols = query_grads.shape
    trains, slots = train_grads.shape[:2]
    queries = n * per
    big = GROUP * rows
    wide = trains // 2
    norm_scale = 1.0 / math.sqrt(slot_total * rows * cols)
    vmem = pl.BlockSpec(memory_space=pltpu.VMEM)
    parts = pl.BlockSpec(memory_space=pltpu.HBM)
    dma = pltpu.SemaphoreType.DMA
    scores = pl.pallas_call(
        functools.partial(kernel, n),
        out_shape=jax.ShapeDtypeStruct((2 * per, trains), F32),
        in_specs=[parts] * 6,
        out_specs=vmem,
        scratch_shapes=[
            pltpu.VMEM(left_basis.shape, BF16),
            pltpu.VMEM(right_basis.shape, BF16),
            pltpu.VMEM(eigenvalues.shape, BF16),
            pltpu.SMEM(block_rows.shape, jnp.int32),
            pltpu.VMEM((slots, queries, rows, cols), BF16),
            pltpu.VMEM((trains, slots, rows, cols), BF16),
            pltpu.VMEM((slots, trains, rows * cols), BF16),
            pltpu.VMEM((slots, 2, queries, rows * cols), BF16),
            pltpu.VMEM((slots, big, big), BF16),
            pltpu.VMEM((slots, big, 2 * cols), F32),
            pltpu.VMEM((2 * queries, trains), F32),
            pltpu.VMEM((4 * queries, 4 * queries), BF16),
            pltpu.VMEM((n, 4 * per, wide), BF16),
            pltpu.VMEM((n, 4 * per, wide), BF16),
            dma((4,)),
            dma,
            dma((slots,)),
            dma((4,)),
            dma((slots,)),
            dma((slots,)),
            dma,
            dma,
        ],
        compiler_params=pltpu.CompilerParams(
            collective_id=0, has_side_effects=True, vmem_limit_bytes=58 * 1024 * 1024
        ),
    )(query_grads, train_grads, left_basis, right_basis, eigenvalues, block_rows)
    return scores * norm_scale


def solution(mesh):
    placed = (
        P(("mod", "pair"), None, None, None),
        P("pair", "mod", None, None),
        P("mod", None, None),
        P("mod", None, None),
        P("mod", None, None),
        P("mod"),
    )
    return jax.shard_map(
        functools.partial(on_device, mesh.shape["mod"]),
        mesh=mesh,
        in_specs=placed,
        out_specs=P("mod", "pair"),
        check_vma=False,
    )
```
